256 devices in a mesh: sub: 32 (over y, z), grp: 8 (over x, core).
Axes of the slice: x: 4, y: 4, z: 8, core: 2. Of those that a mesh axis runs over, the one named last changes fastest.
Arguments:
- stiffness: bfloat16 [32, 128, 5, 256, 256], P('sub', 'grp'), may hold values from -0.0009765625 to 0.0009765625
- deflation: bfloat16 [32, 64, 32768], P('sub', None, 'grp'), may hold values from -6 to 6
- off_map: int32 [32, 3], replicated, may hold values from -2 to 2, as said below
- need_map: int32 [32, 8, 3, 4], P(None, 'grp'), may hold values from 0 to 15, as said below
- place_map: int32 [32, 8, 3, 4], P('sub', 'grp'), may hold values from 0 to 15, as said below
Outputs:
- coarse: float32 [32, 256, 256], P('sub', 'grp')
The draws below stay inside these ranges and needn't reach their ends.
Inputs may be any that keep to these rules, and one draw needn't show every extreme that they name: `off_map`: the 3 offsets of one row are distinct and nonzero. `need_map`: the 4 tile numbers of one row are distinct. `place_map`: the 4 tile numbers of one row are distinct.
All inputs are finite; a program needn't handle non-finite values.
Results may differ from the reference program's by a relative error of at most 0.0029.
Values may be sent and summed in bfloat16 or wider, within the bound.
No kernel may reach another device: no remote copies, remote signals or barrier semaphores. Data moves between devices by JAX's collectives and lax.ppermute only.
A program may use at most 128 MiB of HBM per device.

```python
import jax
import jax.numpy as jnp
from jax import lax

TILE = 256
NVEC = 64
TD = 16
BAND = 5
NB = 3
RCH = 2
OV = 4
NBLK = 4
SUBS = 32
LAYERS = 8
ROWS_SUB = 32768


def pick_distinct(key, count, total, take):
    keys = jax.random.split(key, count)
    perms = jax.vmap(lambda one_key: jax.random.permutation(one_key, total))(keys)
    inner = 1 + jax.random.permutation(jax.random.fold_in(key, 5), total - 2)
    first = jnp.concatenate([jnp.array([0, total - 1], dtype=perms.dtype), inner.astype(perms.dtype)])
    return perms[:, :take].at[0].set(first[:take])


def draw_off_map(key, part):
    picks = pick_distinct(jax.random.fold_in(key, 17), SUBS, 2 * RCH, NB)
    return jnp.where(picks < RCH, picks - RCH, picks - RCH + 1).astype(jnp.int32)


def draw_need_map(key, part):
    picks = pick_distinct(jax.random.fold_in(key, 23), SUBS * LAYERS * NB, TD, OV)
    return picks.reshape(SUBS, LAYERS, NB, OV).astype(jnp.int32)


def draw_place_map(key, part):
    picks = pick_distinct(jax.random.fold_in(key, 29), SUBS * LAYERS * NB, TD, OV)
    return picks.reshape(SUBS, LAYERS, NB, OV).astype(jnp.int32)


def steps_of(stream_key, extent, cuts, least, top_value):
    factor_of, own = 1.0, jax.random.fold_in(stream_key, 6)
    for position, shards_of in cuts:
        steps = jnp.exp(jax.random.uniform(jax.random.fold_in(own, position), (shards_of,), jnp.float32, least / len(cuts), top_value / len(cuts)))
        factor_of = factor_of * jnp.repeat(steps, extent[position] // shards_of).reshape([-1 if axis == position else 1 for axis in range(len(extent))])
    return factor_of


def noise(own_key, dims, deviation, limit, cuts=(), kind=jnp.bfloat16):
    gain = steps_of(own_key, dims, cuts, -0.22, 0.18) if cuts else 1.0
    values = jax.random.normal(own_key, dims, jnp.float32) * deviation * gain
    return jnp.minimum(jnp.maximum(values, -limit), limit).astype(kind)


def setup_inputs(seed: int = 0) -> dict:
    streams_of = jax.random.split(jax.random.key(seed), 6)
    stiffness = noise(streams_of[0], (SUBS, LAYERS * TD, BAND, TILE, TILE), (BAND * TILE * ROWS_SUB) ** -0.5, 0.0009765625, ((0, 32), (1, 8)))
    deflation = noise(streams_of[1], (SUBS, NVEC, ROWS_SUB), 1.0, 6.0, ((0, 32), (2, 8)))
    off_map = draw_off_map(jax.random.fold_in(streams_of[5], 71), 0)
    need_map = draw_need_map(jax.random.fold_in(streams_of[5], 71), 0)
    place_map = draw_place_map(jax.random.fold_in(streams_of[5], 71), 0)
    return {"stiffness": stiffness, "deflation": deflation, "off_map": off_map, "need_map": need_map, "place_map": place_map}


def reference(stiffness, deflation, off_map, need_map, place_map):
    rim_tiles = BAND // 2
    all_tiles = LAYERS * TD
    basis_tiles = deflation.reshape(SUBS, NVEC, LAYERS, TD, TILE)
    layer_ids = jnp.arange(LAYERS, dtype=jnp.int32)[:, None]

    def subdomain_block(subdomain):
        own_basis = basis_tiles[subdomain]
        blocks = [own_basis]
        for slot_index in range(NB):
            other = jnp.mod(subdomain + off_map[subdomain, slot_index], SUBS).astype(jnp.int32)
            source = basis_tiles[other]
            needed = need_map[subdomain, :, slot_index, :]
            placed = place_map[subdomain, :, slot_index, :]
            picked = source[:, layer_ids, needed, :]
            blank_tiles = jnp.zeros_like(own_basis)
            blocks.append(blank_tiles.at[:, layer_ids, placed, :].set(picked))
        basis = jnp.concatenate(blocks, 0).reshape(NBLK * NVEC, all_tiles, TILE)
        padded = jnp.pad(basis, ((0, 0), (rim_tiles, rim_tiles), (0, 0))).astype(jnp.float32)
        local_stiffness = stiffness[subdomain]
        running = jnp.zeros((NBLK * NVEC, all_tiles, TILE), jnp.float32)
        for band_index in range(BAND):
            window = padded[:, band_index:band_index + all_tiles]
            tiles_now = local_stiffness[:, band_index].astype(jnp.float32)
            running = running + jnp.einsum("ctk,tjk->ctj", window, tiles_now)
        product_image = running.astype(jnp.bfloat16)
        flat_basis = basis.reshape(NBLK * NVEC, all_tiles * TILE)
        flat_image = product_image.reshape(NBLK * NVEC, all_tiles * TILE)
        return jnp.dot(flat_basis, flat_image.T, preferred_element_type=jnp.float32)

    return lax.map(subdomain_block, jnp.arange(SUBS, dtype=jnp.int32))
```

```python
import jax
import jax.numpy as jnp
from jax import lax
from jax.experimental import pallas as pl
from jax.experimental.pallas import tpu as pltpu
from jax.sharding import PartitionSpec as P

SUBS = 32
LAYERS = 8
TILE = 256
TD = 16
NVEC = 64
NB = 3
OV = 4
BAND = 5
RIM = BAND // 2
COLS = 256
REST = NB * NVEC
SHIFTS = (2, 1, -1, -2)
SMEM = pl.BlockSpec(memory_space=pltpu.SMEM)
VMEM = pl.BlockSpec(memory_space=pltpu.VMEM)
HBM = pl.BlockSpec(memory_space=pltpu.HBM)
NT = (((1,), (1,)), ((), ()))
bf16, f32 = jnp.bfloat16, jnp.float32


def kernel_call(body, out_shape, specs, scratch=(), mib=4, flops=0, size=0):
    return pl.pallas_call(
        body,
        out_shape=out_shape,
        in_specs=specs,
        out_specs=jax.tree.map(lambda _: VMEM, out_shape),
        scratch_shapes=scratch,
        compiler_params=pltpu.CompilerParams(vmem_limit_bytes=mib * 2**20),
        cost_estimate=pl.CostEstimate(flops=flops, bytes_accessed=size, transcendentals=0),
    )


def lanes(tile, count=1):
    return pl.ds(pl.multiple_of(tile * TILE, TILE), count * TILE)


def tile_of(ref, c):
    return ref[:, c * TILE : (c + 1) * TILE]


def row_sum(ref, stiff, c):
    total = None
    for t in range(max(0, c - RIM), min(TD, c + RIM + 1)):
        term = jnp.dot(tile_of(ref, t), stiff[t, c - t + RIM], preferred_element_type=f32)
        total = term if total is None else total + term
    return total


def pack_kernel(off_hbm, need_hbm, own_hbm, *refs):
    outs, (off_ref, need_ref, own_ref, sems) = refs[:4], refs[4:]
    copies = [
        pltpu.make_async_copy(source, target, sems.at[i])
        for i, (source, target) in enumerate(
            ((off_hbm, off_ref), (need_hbm, need_ref), (own_hbm, own_ref))
        )
    ]
    for copy in copies:
        copy.start()
    for copy in copies:
        copy.wait()
    me = lax.axis_index("sub")
    for shift, out in zip(SHIFTS, outs):
        target = lax.rem(me + (shift + SUBS), SUBS)
        slot = jnp.where(
            off_ref[0, target] == -shift, 0, jnp.where(off_ref[1, target] == -shift, 1, 2)
        )
        for o in range(OV):
            out[:, o * TILE : (o + 1) * TILE] = own_ref[:, lanes(need_ref[slot, o, target])]


def own_kernel(stiff, own, product):
    for c in range(-RIM, TD + RIM):
        product[:, (c + RIM) * TILE : (c + RIM + 1) * TILE] = row_sum(own, stiff, c).astype(bf16)


def edge_kernel(off_ref, place_ref, own, *refs):
    arrived, (near, far, sides) = refs[:4], refs[4:]
    me = lax.axis_index("sub")
    odd = lax.rem(lax.axis_index("grp"), 2)
    sides[:, NVEC:] = jnp.zeros((2, REST, RIM * TILE), bf16)
    sides[1 - odd, :NVEC] = own[:, : RIM * TILE]
    sides[odd, :NVEC] = own[:, (TD - RIM) * TILE :]
    for shift, block in zip(SHIFTS, arrived):
        first, second, third = (off_ref[slot, me] == -shift for slot in range(NB))
        slot = jnp.where(first, 0, jnp.where(second, 1, 2))
        used = jnp.logical_or(first, jnp.logical_or(second, third))
        rows = pl.ds(pl.multiple_of((slot + 1) * NVEC, NVEC), NVEC)
        for o in range(OV):
            tile = place_ref[slot, 0, o]
            low, high = tile < RIM, tile >= TD - RIM

            @pl.when(jnp.logical_and(used, jnp.logical_or(low, high)))
            def _():
                side = jnp.where(low, 1 - odd, odd)
                sides[side, rows, lanes(jnp.where(low, tile, tile - (TD - RIM)))] = tile_of(
                    block, o
                )

    near[...] = sides[0]
    far[...] = sides[1]


def main_kernel(off_ref, place_ref, stiff, own, product, *refs):
    arrived, (total, carry, basis, rows) = refs[:4], refs[4:]
    me = lax.axis_index("sub")
    basis[:NVEC] = own[...]
    basis[NVEC:] = jnp.zeros((REST, TD * TILE), bf16)
    for shift, block in zip(SHIFTS, arrived):
        for slot in range(NB):

            @pl.when(off_ref[slot, me] == -shift)
            def _():
                for o in range(OV):
                    tile = place_ref[slot, 0, o]
                    basis[(slot + 1) * NVEC : (slot + 2) * NVEC, lanes(tile)] = tile_of(block, o)

    others = basis.at[NVEC:]
    rows[:NVEC] = product[:, RIM * TILE : (RIM + TD) * TILE]
    for c in range(TD):
        rows[NVEC:, c * TILE : (c + 1) * TILE] = row_sum(others, stiff, c).astype(bf16)
    total[...] = lax.dot_general(rows[...], basis[...], NT, preferred_element_type=f32)
    carry[:NVEC, : RIM * TILE] = product[:, : RIM * TILE]
    carry[:NVEC, RIM * TILE :] = product[:, (RIM + TD) * TILE :]
    for i, c in enumerate((-2, -1, TD, TD + 1)):
        carry[NVEC:, i * TILE : (i + 1) * TILE] = row_sum(others, stiff, c).astype(bf16)


def finish_kernel(total, carry, near, far, mine, other, sums):
    odd = lax.rem(lax.axis_index("grp"), 2)

    def outer(side, right):
        half = RIM * TILE
        left = carry[:, pl.ds(pl.multiple_of(side * half, half), half)]
        return lax.dot_general(left, right[...], NT, preferred_element_type=f32)

    sums[...] = total[...] + outer(1 - odd, near) + outer(odd, far)
    share = COLS // LAYERS
    for x in range(LAYERS // 2):
        mine[x] = sums[pl.ds(pl.multiple_of((2 * x + odd) * share, share), share)]
        other[x] = sums[pl.ds(pl.multiple_of((2 * x + 1 - odd) * share, share), share)]


def swapped(value, pairs):
    return lax.ppermute(value, "grp", [p for a, b in pairs for p in ((a, b), (b, a))])


def on_device(stiffness, deflation, off_map, need_map, place_map):
    stiff, own = stiffness[0], deflation[0]
    off = off_map.T
    need = need_map.transpose(1, 2, 3, 0)[0]
    place = place_map[0].transpose(1, 0, 2)
    shape = jax.ShapeDtypeStruct

    packed = kernel_call(
        pack_kernel,
        [shape((NVEC, OV * TILE), bf16)] * 4,
        [HBM] * 3,
        [
            pltpu.SMEM(off.shape, jnp.int32),
            pltpu.SMEM(need.shape, jnp.int32),
            pltpu.VMEM(own.shape, bf16),
            pltpu.SemaphoreType.DMA((3,)),
        ],
    )(off, need, own)
    arrived = [
        lax.ppermute(block, "sub", [(k, (k + shift) % SUBS) for k in range(SUBS)])
        for shift, block in zip(SHIFTS, packed)
    ]
    product = kernel_call(
        own_kernel,
        shape((NVEC, (TD + 2 * RIM) * TILE), bf16),
        [VMEM, VMEM],
        mib=16,
        flops=2 * NVEC * TD * BAND * TILE * TILE,
        size=2**20,
    )(stiff, own)
    edges = shape((COLS, RIM * TILE), bf16)
    near, far = kernel_call(
        edge_kernel,
        [edges, edges],
        [SMEM, SMEM] + [VMEM] * 5,
        [pltpu.VMEM((2, COLS, RIM * TILE), bf16)],
    )(off, place, own, *arrived)
    near = swapped(near, [(k, k + 1) for k in range(0, LAYERS, 2)])
    far = swapped(far, [(k, k + 1) for k in range(1, LAYERS - 1, 2)])
    total, carry = kernel_call(
        main_kernel,
        [shape((COLS, COLS), f32), shape((COLS, 2 * RIM * TILE), bf16)],
        [SMEM, SMEM] + [VMEM] * 7,
        [pltpu.VMEM((COLS, TD * TILE), bf16), pltpu.VMEM((COLS, TD * TILE), bf16)],
        mib=24,
        flops=2 * COLS * TD * (BAND + 1) * TILE * TILE,
        size=2**22,
    )(off, place, stiff, own, product, *arrived)
    part = shape((LAYERS // 2, COLS // LAYERS, COLS), f32)
    mine, other = kernel_call(
        finish_kernel, [part, part], [VMEM] * 4, [pltpu.VMEM((COLS, COLS), f32)]
    )(total, carry, near, far)
    both = mine + lax.ppermute(other, "grp", [(k, k ^ 1) for k in range(LAYERS)])
    chip = lax.shift_right_logical(lax.axis_index("grp"), 1)
    share = lax.dynamic_index_in_dim(both, chip, 0, keepdims=False)
    for step in (1, 3, 2):
        block = lax.dynamic_index_in_dim(both, chip ^ step, 0, keepdims=False)
        share = share + lax.ppermute(block, "grp", [(k, k ^ (2 * step)) for k in range(LAYERS)])
    return share[None]


def solution(mesh):
    in_specs = (
        P("sub", "grp", None, None, None),
        P("sub", None, "grp"),
        P(),
        P(None, "grp", None, None),
        P("sub", "grp", None, None),
    )
    out_specs = P("sub", "grp", None)
    return jax.shard_map(
        on_device, mesh=mesh, in_specs=in_specs, out_specs=out_specs, check_vma=False
    )
```

```python
import jax
import jax.numpy as jnp
from jax import lax
from jax.experimental import pallas as pl
from jax.experimental.pallas import tpu as pltpu
from jax.sharding import PartitionSpec as P

SUBS = 32
LAYERS = 8
TILE = 256
TD = 16
NVEC = 64
NB = 3
OV = 4
BAND = 5
RIM = BAND // 2
COLS = 256
REST = NB * NVEC
AHEAD = 8
SHIFTS = (2, 1, -1, -2)
SMEM = pl.BlockSpec(memory_space=pltpu.SMEM)
VMEM = pl.BlockSpec(memory_space=pltpu.VMEM)
HBM = pl.BlockSpec(memory_space=pltpu.HBM)
NT = (((1,), (1,)), ((), ()))
bf16, f32 = jnp.bfloat16, jnp.float32


def kernel_call(body, out_shape, specs, scratch=(), mib=4, flops=0, size=0):
    return pl.pallas_call(
        body,
        out_shape=out_shape,
        in_specs=specs,
        out_specs=[VMEM] * len(out_shape),
        scratch_shapes=scratch,
        compiler_params=pltpu.CompilerParams(vmem_limit_bytes=mib * 2**20),
        cost_estimate=pl.CostEstimate(flops=flops, bytes_accessed=size, transcendentals=0),
    )


def lanes(tile, count=1):
    return pl.ds(pl.multiple_of(tile * TILE, TILE), count * TILE)


def tile_of(ref, c):
    return ref[:, c * TILE : (c + 1) * TILE]


def row_sum(ref, stiff, c):
    total = None
    for t in range(max(0, c - RIM), min(TD, c + RIM + 1)):
        term = jnp.dot(tile_of(ref, t), stiff[t, c - t + RIM], preferred_element_type=f32)
        total = term if total is None else total + term
    return total


def pack_kernel(off_hbm, need_hbm, own_hbm, *refs):
    outs, (own_ref, off_ref, need_ref, sems) = refs[:4], refs[4:]
    copies = [
        pltpu.make_async_copy(source, target, sems.at[i])
        for i, (source, target) in enumerate(
            ((off_hbm, off_ref), (need_hbm, need_ref), (own_hbm, own_ref))
        )
    ]
    for copy in copies:
        copy.start()
    for copy in copies:
        copy.wait()
    me = lax.axis_index("sub")
    for shift, out in zip(SHIFTS, outs):
        target = lax.rem(me + (shift + SUBS), SUBS)
        slot = jnp.where(
            off_ref[0, target] == -shift, 0, jnp.where(off_ref[1, target] == -shift, 1, 2)
        )
        for o in range(OV):
            out[:, o * TILE : (o + 1) * TILE] = own_ref[:, lanes(need_ref[slot, o, target])]


def own_kernel(stiff_hbm, own, product, stiff, sems):
    copies = [
        pltpu.make_async_copy(stiff_hbm.at[t], stiff.at[t], sems.at[t]) for t in range(TD)
    ]
    for copy in copies[:AHEAD]:
        copy.start()
    for c in range(-RIM, TD + RIM):
        if c + RIM < TD:
            copies[c + RIM].wait()
            if c + RIM + AHEAD < TD:
                copies[c + RIM + AHEAD].start()
        product[:, (c + RIM) * TILE : (c + RIM + 1) * TILE] = row_sum(own, stiff, c).astype(bf16)


def edge_kernel(off_ref, place_ref, own, *refs):
    arrived, (near, far, sides) = refs[:4], refs[4:]
    me = lax.axis_index("sub")
    odd = lax.rem(lax.axis_index("grp"), 2)
    sides[:, NVEC:] = jnp.zeros((2, REST, RIM * TILE), bf16)
    sides[1 - odd, :NVEC] = own[:, : RIM * TILE]
    sides[odd, :NVEC] = own[:, (TD - RIM) * TILE :]
    for shift, block in zip(SHIFTS, arrived):
        first, second, third = (off_ref[slot, me] == -shift for slot in range(NB))
        slot = jnp.where(first, 0, jnp.where(second, 1, 2))
        used = jnp.logical_or(first, jnp.logical_or(second, third))
        rows = pl.ds(pl.multiple_of((slot + 1) * NVEC, NVEC), NVEC)
        for o in range(OV):
            tile = place_ref[slot, 0, o]
            low, high = tile < RIM, tile >= TD - RIM

            @pl.when(jnp.logical_and(used, jnp.logical_or(low, high)))
            def _():
                side = jnp.where(low, 1 - odd, odd)
                sides[side, rows, lanes(jnp.where(low, tile, tile - (TD - RIM)))] = tile_of(
                    block, o
                )

    near[...] = sides[0]
    far[...] = sides[1]


def main_kernel(off_ref, place_ref, stiff, own, product, *refs):
    arrived, (total, carry, basis, rows) = refs[:4], refs[4:]
    me = lax.axis_index("sub")
    basis[:NVEC] = own[...]
    basis[NVEC:] = jnp.zeros((REST, TD * TILE), bf16)
    for shift, block in zip(SHIFTS, arrived):
        for slot in range(NB):

            @pl.when(off_ref[slot, me] == -shift)
            def _():
                for o in range(OV):
                    tile = place_ref[slot, 0, o]
                    basis[(slot + 1) * NVEC : (slot + 2) * NVEC, lanes(tile)] = tile_of(block, o)

    others = basis.at[NVEC:]
    rows[:NVEC] = product[:, RIM * TILE : (RIM + TD) * TILE]
    for c in range(TD):
        rows[NVEC:, c * TILE : (c + 1) * TILE] = row_sum(others, stiff, c).astype(bf16)
    total[...] = lax.dot_general(rows[...], basis[...], NT, preferred_element_type=f32)
    carry[:NVEC, : RIM * TILE] = product[:, : RIM * TILE]
    carry[:NVEC, RIM * TILE :] = product[:, (RIM + TD) * TILE :]
    for i, c in enumerate((-2, -1, TD, TD + 1)):
        carry[NVEC:, i * TILE : (i + 1) * TILE] = row_sum(others, stiff, c).astype(bf16)


def finish_kernel(total, carry, far, near, mine, other, sums):
    layer = lax.axis_index("grp")
    odd = lax.rem(layer, 2)
    inner = jnp.logical_and(layer > 0, layer < LAYERS - 1)

    def outer(side, right):
        half = RIM * TILE
        left = carry[:, pl.ds(pl.multiple_of(side * half, half), half)]
        return lax.dot_general(left, right[...], NT, preferred_element_type=f32)

    sums[...] = total[...] + outer(1 - odd, near)

    @pl.when(inner)
    def _():
        sums[...] += outer(odd, far)

    share = COLS // LAYERS
    for x in range(LAYERS // 2):
        mine[x] = sums[pl.ds(pl.multiple_of((2 * x + odd) * share, share), share)]
        other[x] = sums[pl.ds(pl.multiple_of((2 * x + 1 - odd) * share, share), share)]


def swapped(value, pairs):
    return lax.ppermute(value, "grp", [p for a, b in pairs for p in ((a, b), (b, a))])


def on_device(stiffness, deflation, off_map, need_map, place_map):
    stiff, own = stiffness[0], deflation[0]
    off = off_map.T
    need = need_map.transpose(1, 2, 3, 0)[0]
    place = place_map[0].transpose(1, 0, 2)
    shape = jax.ShapeDtypeStruct

    *packed, own = kernel_call(
        pack_kernel,
        [shape((NVEC, OV * TILE), bf16)] * 4 + [pltpu.VMEM(own.shape, bf16)],
        [HBM] * 3,
        [
            pltpu.SMEM(off.shape, jnp.int32),
            pltpu.SMEM(need.shape, jnp.int32),
            pltpu.SemaphoreType.DMA((3,)),
        ],
    )(*(pltpu.with_memory_space_constraint(value, pltpu.HBM) for value in (off, need, own)))
    own = pltpu.with_memory_space_constraint(own, pltpu.VMEM)
    arrived = [
        lax.ppermute(block, "sub", [(k, (k + shift) % SUBS) for k in range(SUBS)])
        for shift, block in zip(SHIFTS, packed)
    ]
    product, stiff = kernel_call(
        own_kernel,
        [shape((NVEC, (TD + 2 * RIM) * TILE), bf16), pltpu.VMEM(stiff.shape, bf16)],
        [HBM, VMEM],
        [pltpu.SemaphoreType.DMA((TD,))],
        mib=4,
        flops=2 * NVEC * TD * BAND * TILE * TILE,
        size=2**24,
    )(pltpu.with_memory_space_constraint(stiff, pltpu.HBM), own)
    stiff = pltpu.with_memory_space_constraint(stiff, pltpu.VMEM)
    edges = shape((COLS, RIM * TILE), bf16)
    near, far = kernel_call(
        edge_kernel,
        [edges, edges],
        [SMEM, SMEM] + [VMEM] * 5,
        [pltpu.VMEM((2, COLS, RIM * TILE), bf16)],
    )(off, place, own, *arrived)
    far = swapped(far, [(k, (k + 1) % LAYERS) for k in range(1, LAYERS, 2)])
    near = swapped(near, [(k, k + 1) for k in range(0, LAYERS, 2)])
    total, carry = kernel_call(
        main_kernel,
        [shape((COLS, COLS), f32), shape((COLS, 2 * RIM * TILE), bf16)],
        [SMEM, SMEM] + [VMEM] * 7,
        [pltpu.VMEM((COLS, TD * TILE), bf16), pltpu.VMEM((COLS, TD * TILE), bf16)],
        mib=24,
        flops=2 * COLS * TD * (BAND + 1) * TILE * TILE,
        size=2**22,
    )(off, place, stiff, own, product, *arrived)
    part = shape((LAYERS // 2, COLS // LAYERS, COLS), f32)
    mine, other = kernel_call(
        finish_kernel, [part, part], [VMEM] * 4, [pltpu.VMEM((COLS, COLS), f32)]
    )(total, carry, far, near)
    both = mine + lax.ppermute(other, "grp", [(k, k ^ 1) for k in range(LAYERS)])
    chip = lax.shift_right_logical(lax.axis_index("grp"), 1)
    share = lax.dynamic_index_in_dim(both, chip, 0, keepdims=False)
    for step in (2, 3, 1):
        block = lax.dynamic_index_in_dim(both, chip ^ step, 0, keepdims=False)
        share = share + lax.ppermute(block, "grp", [(k, k ^ (2 * step)) for k in range(LAYERS)])
    return share[None]


def solution(mesh):
    in_specs = (
        P("sub", "grp", None, None, None),
        P("sub", None, "grp"),
        P(),
        P(None, "grp", None, None),
        P("sub", "grp", None, None),
    )
    out_specs = P("sub", "grp", None)
    return jax.shard_map(
        on_device, mesh=mesh, in_specs=in_specs, out_specs=out_specs, check_vma=False
    )
```

```python
import jax
import jax.numpy as jnp
from jax import lax
from jax.experimental import pallas as pl
from jax.experimental.pallas import tpu as pltpu
from jax.sharding import PartitionSpec as P

SUBS = 32
LAYERS = 8
TILE = 256
TD = 16
NVEC = 64
NB = 3
OV = 4
BAND = 5
RIM = BAND // 2
COLS = 256
REST = NB * NVEC
AHEAD = 8
SHIFTS = (2, 1, -2, -1)
SMEM = pl.BlockSpec(memory_space=pltpu.SMEM)
VMEM = pl.BlockSpec(memory_space=pltpu.VMEM)
HBM = pl.BlockSpec(memory_space=pltpu.HBM)
NT = (((1,), (1,)), ((), ()))
bf16, f32 = jnp.bfloat16, jnp.float32


def kernel_call(body, out_shape, specs, scratch=(), mib=4, flops=0, size=0, aliases=None):
    return pl.pallas_call(
        body,
        out_shape=out_shape,
        in_specs=specs,
        out_specs=[VMEM] * len(out_shape),
        scratch_shapes=scratch,
        input_output_aliases=aliases or {},
        compiler_params=pltpu.CompilerParams(vmem_limit_bytes=mib * 2**20),
        cost_estimate=pl.CostEstimate(flops=flops, bytes_accessed=size, transcendentals=0),
    )


def lanes(tile, count=1):
    return pl.ds(pl.multiple_of(tile * TILE, TILE), count * TILE)


def tile_of(ref, c):
    return ref[:, c * TILE : (c + 1) * TILE]


def row_sum(ref, stiff, c):
    total = None
    for t in range(max(0, c - RIM), min(TD, c + RIM + 1)):
        term = jnp.dot(tile_of(ref, t), stiff[t, c - t + RIM], preferred_element_type=f32)
        total = term if total is None else total + term
    return total


def pack_kernel(off_hbm, need_hbm, own_hbm, *refs):
    outs, (own_ref, off_ref, need_ref, sems) = refs[:4], refs[4:]
    copies = [
        pltpu.make_async_copy(source, target, sems.at[i])
        for i, (source, target) in enumerate(
            ((off_hbm, off_ref), (need_hbm, need_ref), (own_hbm, own_ref))
        )
    ]
    for copy in copies:
        copy.start()
    for copy in copies:
        copy.wait()
    me = lax.axis_index("sub")
    for shift, out in zip(SHIFTS, outs):
        target = lax.rem(me + (shift + SUBS), SUBS)
        slot = jnp.where(
            off_ref[0, target] == -shift, 0, jnp.where(off_ref[1, target] == -shift, 1, 2)
        )
        for o in range(OV):
            out[:, o * TILE : (o + 1) * TILE] = own_ref[:, lanes(need_ref[slot, o, target])]


def split(value):
    first = value.astype(bf16)
    return first, (value - first.astype(f32)).astype(bf16)


def own_kernel(stiff_hbm, own, product, rest, stiff, basis, near, far, sems):
    copies = [
        pltpu.make_async_copy(stiff_hbm.at[t], stiff.at[t], sems.at[t]) for t in range(TD)
    ]
    for copy in copies[:AHEAD]:
        copy.start()
    odd = lax.rem(lax.axis_index("grp"), 2)
    basis[:NVEC] = own[...]
    basis[NVEC:] = jnp.zeros((REST, TD * TILE), bf16)
    for ref, first in ((near, (1 - odd) * (TD - RIM)), (far, odd * (TD - RIM))):
        ref[:NVEC] = own[:, lanes(first, RIM)]
        ref[NVEC:] = jnp.zeros((REST, RIM * TILE), bf16)
    for c in range(-RIM, TD + RIM):
        if c + RIM < TD:
            copies[c + RIM].wait()
            if c + RIM + AHEAD < TD:
                copies[c + RIM + AHEAD].start()
        first, second = split(row_sum(own, stiff, c))
        product[:, (c + RIM) * TILE : (c + RIM + 1) * TILE] = first
        if 0 <= c < TD:
            rest[:, c * TILE : (c + 1) * TILE] = second


def edge_kernel(off_ref, place_ref, *refs):
    arrived, (near, far) = refs[2:6], refs[6:]
    me = lax.axis_index("sub")
    odd = lax.rem(lax.axis_index("grp"), 2) == 1
    for shift, block in zip(SHIFTS, arrived):
        first, second, third = (off_ref[slot, me] == -shift for slot in range(NB))
        slot = jnp.where(first, 0, jnp.where(second, 1, 2))
        used = jnp.logical_or(first, jnp.logical_or(second, third))
        rows = pl.ds(pl.multiple_of((slot + 1) * NVEC, NVEC), NVEC)
        for o in range(OV):
            tile = place_ref[slot, 0, o]
            low, high = tile < RIM, tile >= TD - RIM
            spot = lanes(jnp.where(low, tile, tile - (TD - RIM)))
            rim = jnp.logical_and(used, jnp.logical_or(low, high))

            @pl.when(jnp.logical_and(rim, low == odd))
            def _():
                near[rows, spot] = tile_of(block, o)

            @pl.when(jnp.logical_and(rim, low != odd))
            def _():
                far[rows, spot] = tile_of(block, o)


def main_kernel(off_ref, place_ref, stiff, product, rest, _, *refs):
    arrived, (total, carry, basis, rows, low_rows) = refs[:4], refs[4:]
    me = lax.axis_index("sub")
    for shift, block in zip(SHIFTS, arrived):
        for slot in range(NB):

            @pl.when(off_ref[slot, me] == -shift)
            def _():
                for o in range(OV):
                    tile = place_ref[slot, 0, o]
                    basis[(slot + 1) * NVEC : (slot + 2) * NVEC, lanes(tile)] = tile_of(block, o)

    others = basis.at[NVEC:]
    rows[:NVEC] = product[:, RIM * TILE : (RIM + TD) * TILE]
    low_rows[:NVEC] = rest[...]
    for c in range(TD):
        first, second = split(row_sum(others, stiff, c))
        rows[NVEC:, c * TILE : (c + 1) * TILE] = first
        low_rows[NVEC:, c * TILE : (c + 1) * TILE] = second
    total[...] = lax.dot_general(
        rows[...], basis[...], NT, preferred_element_type=f32
    ) + lax.dot_general(low_rows[...], basis[...], NT, preferred_element_type=f32)
    carry[:NVEC, : RIM * TILE] = product[:, : RIM * TILE]
    carry[:NVEC, RIM * TILE :] = product[:, (RIM + TD) * TILE :]
    for i, c in enumerate((-2, -1, TD, TD + 1)):
        carry[NVEC:, i * TILE : (i + 1) * TILE] = row_sum(others, stiff, c).astype(bf16)


def finish_kernel(total, carry, far, near, mine, other, sums):
    layer = lax.axis_index("grp")
    odd = lax.rem(layer, 2)
    inner = jnp.logical_and(layer > 0, layer < LAYERS - 1)

    def outer(side, right):
        half = RIM * TILE
        left = carry[:, pl.ds(pl.multiple_of(side * half, half), half)]
        return lax.dot_general(left, right[...], NT, preferred_element_type=f32)

    sums[...] = total[...] + outer(1 - odd, near)

    @pl.when(inner)
    def _():
        sums[...] += outer(odd, far)

    share = COLS // LAYERS
    for x in range(LAYERS // 2):
        mine[x] = sums[pl.ds(pl.multiple_of((2 * x + odd) * share, share), share)]
        other[x] = sums[pl.ds(pl.multiple_of((2 * x + 1 - odd) * share, share), share)]


def far_moves():
    moves = []
    for sub in range(SUBS):
        for layer in range(LAYERS):
            if layer in (0, LAYERS - 1):
                to = (sub ^ 1, layer)
            else:
                to = (sub, layer + 1 if layer % 2 else layer - 1)
            moves.append((sub * LAYERS + layer, to[0] * LAYERS + to[1]))
    return moves


def swapped(value, pairs):
    return lax.ppermute(value, "grp", [p for a, b in pairs for p in ((a, b), (b, a))])


def on_device(stiffness, deflation, off_map, need_map, place_map):
    stiff, own = stiffness[0], deflation[0]
    off = off_map.T
    need = need_map.transpose(1, 2, 3, 0)[0]
    place = place_map[0].transpose(1, 0, 2)
    shape = jax.ShapeDtypeStruct

    *packed, own = kernel_call(
        pack_kernel,
        [shape((NVEC, OV * TILE), bf16)] * 4 + [pltpu.VMEM(own.shape, bf16)],
        [HBM] * 3,
        [
            pltpu.SMEM(off.shape, jnp.int32),
            pltpu.SMEM(need.shape, jnp.int32),
            pltpu.SemaphoreType.DMA((3,)),
        ],
    )(*(pltpu.with_memory_space_constraint(value, pltpu.HBM) for value in (off, need, own)))
    own = pltpu.with_memory_space_constraint(own, pltpu.VMEM)
    arrived = [
        lax.ppermute(block, "sub", [(k, (k + shift) % SUBS) for k in range(SUBS)])
        for shift, block in zip(SHIFTS, packed)
    ]
    edges = pltpu.VMEM((COLS, RIM * TILE), bf16)
    whole = pltpu.VMEM((COLS, TD * TILE), bf16)
    product, rest, *kept = kernel_call(
        own_kernel,
        [
            shape((NVEC, (TD + 2 * RIM) * TILE), bf16),
            shape((NVEC, TD * TILE), bf16),
            pltpu.VMEM(stiff.shape, bf16),
            whole,
            edges,
            edges,
        ],
        [HBM, VMEM],
        [pltpu.SemaphoreType.DMA((TD,))],
        flops=2 * NVEC * TD * BAND * TILE * TILE,
        size=2**24,
    )(pltpu.with_memory_space_constraint(stiff, pltpu.HBM), own)
    stiff, basis, near, far = (
        pltpu.with_memory_space_constraint(value, pltpu.VMEM) for value in kept
    )
    near, far = kernel_call(
        edge_kernel,
        [shape((COLS, RIM * TILE), bf16)] * 2,
        [SMEM, SMEM] + [VMEM] * 6,
        aliases={2: 0, 3: 1},
    )(off, place, near, far, *arrived)
    far = lax.ppermute(far, ("sub", "grp"), far_moves())
    near = swapped(near, [(k, k + 1) for k in range(0, LAYERS, 2)])
    total, carry, _ = kernel_call(
        main_kernel,
        [
            shape((COLS, COLS), f32),
            shape((COLS, 2 * RIM * TILE), bf16),
            shape((COLS, TD * TILE), bf16),
        ],
        [SMEM, SMEM] + [VMEM] * 8,
        [pltpu.VMEM((COLS, TD * TILE), bf16)] * 2,
        mib=24,
        flops=2 * COLS * TD * (BAND + 1) * TILE * TILE,
        size=2**22,
        aliases={5: 2},
    )(off, place, stiff, product, rest, basis, *arrived)
    part = shape((LAYERS // 2, COLS // LAYERS, COLS), f32)
    mine, other = kernel_call(
        finish_kernel, [part, part], [VMEM] * 4, [pltpu.VMEM((COLS, COLS), f32)]
    )(total, carry, far, near)
    both = mine + lax.ppermute(other, "grp", [(k, k ^ 1) for k in range(LAYERS)])
    chip = lax.shift_right_logical(lax.axis_index("grp"), 1)
    share = lax.dynamic_index_in_dim(both, chip, 0, keepdims=False)
    for step in (2, 3, 1):
        block = lax.dynamic_index_in_dim(both, chip ^ step, 0, keepdims=False)
        share = share + lax.ppermute(block, "grp", [(k, k ^ (2 * step)) for k in range(LAYERS)])
    return share[None]


def solution(mesh):
    in_specs = (
        P("sub", "grp", None, None, None),
        P("sub", None, "grp"),
        P(),
        P(None, "grp", None, None),
        P("sub", "grp", None, None),
    )
    out_specs = P("sub", "grp", None)
    return jax.shard_map(
        on_device, mesh=mesh, in_specs=in_specs, out_specs=out_specs, check_vma=False
    )
```

```python
import jax
import jax.numpy as jnp
from jax import lax
from jax.experimental import pallas as pl
from jax.experimental.pallas import tpu as pltpu
from jax.sharding import PartitionSpec as P

SUBS = 32
LAYERS = 8
TILE = 256
TD = 16
NVEC = 64
NB = 3
OV = 4
BAND = 5
RIM = BAND // 2
COLS = 256
REST = NB * NVEC
AHEAD = 8
SHIFTS = (1, 2, -2, -1)
SMEM = pl.BlockSpec(memory_space=pltpu.SMEM)
VMEM = pl.BlockSpec(memory_space=pltpu.VMEM)
HBM = pl.BlockSpec(memory_space=pltpu.HBM)
NT = (((1,), (1,)), ((), ()))
bf16, f32 = jnp.bfloat16, jnp.float32


def kernel_call(body, out_shape, specs, scratch=(), mib=4, flops=0, size=0, aliases=None):
    return pl.pallas_call(
        body,
        out_shape=out_shape,
        in_specs=specs,
        out_specs=[VMEM] * len(out_shape),
        scratch_shapes=scratch,
        input_output_aliases=aliases or {},
        compiler_params=pltpu.CompilerParams(vmem_limit_bytes=mib * 2**20),
        cost_estimate=pl.CostEstimate(flops=flops, bytes_accessed=size, transcendentals=0),
    )


def lanes(tile, count=1):
    return pl.ds(pl.multiple_of(tile * TILE, TILE), count * TILE)


def tile_of(ref, c):
    return ref[:, c * TILE : (c + 1) * TILE]


def row_sum(ref, stiff, c):
    total = None
    for t in range(max(0, c - RIM), min(TD, c + RIM + 1)):
        term = jnp.dot(tile_of(ref, t), stiff[t, c - t + RIM], preferred_element_type=f32)
        total = term if total is None else total + term
    return total


def pack_kernel(off_hbm, need_hbm, own_hbm, *refs):
    outs, (own_ref, off_ref, need_ref, sems) = refs[:4], refs[4:]
    copies = [
        pltpu.make_async_copy(source, target, sems.at[i])
        for i, (source, target) in enumerate(
            ((off_hbm, off_ref), (need_hbm, need_ref), (own_hbm, own_ref))
        )
    ]
    for copy in copies:
        copy.start()
    for copy in copies:
        copy.wait()
    me = lax.axis_index("sub")
    for shift, out in zip(SHIFTS, outs):
        target = lax.rem(me + (shift + SUBS), SUBS)
        slot = jnp.where(
            off_ref[0, target] == -shift, 0, jnp.where(off_ref[1, target] == -shift, 1, 2)
        )
        for o in range(OV):
            out[:, o * TILE : (o + 1) * TILE] = own_ref[:, lanes(need_ref[slot, o, target])]


def split(value):
    first = value.astype(bf16)
    return first, (value - first.astype(f32)).astype(bf16)


def own_kernel(stiff_hbm, own, product, rest, stiff, basis, near, far, sems):
    copies = [
        pltpu.make_async_copy(stiff_hbm.at[t], stiff.at[t], sems.at[t]) for t in range(TD)
    ]
    for copy in copies[:AHEAD]:
        copy.start()
    odd = lax.rem(lax.axis_index("grp"), 2)
    basis[:NVEC] = own[...]
    basis[NVEC:] = jnp.zeros((REST, TD * TILE), bf16)
    for ref, first in ((near, (1 - odd) * (TD - RIM)), (far, odd * (TD - RIM))):
        ref[:NVEC] = own[:, lanes(first, RIM)]
        ref[NVEC:] = jnp.zeros((REST, RIM * TILE), bf16)
    for c in range(-RIM, TD + RIM):
        if c + RIM < TD:
            copies[c + RIM].wait()
            if c + RIM + AHEAD < TD:
                copies[c + RIM + AHEAD].start()
        first, second = split(row_sum(own, stiff, c))
        product[:, (c + RIM) * TILE : (c + RIM + 1) * TILE] = first
        if 0 <= c < TD:
            rest[:, c * TILE : (c + 1) * TILE] = second


def edge_kernel(off_ref, place_ref, *refs):
    arrived, (near, far) = refs[2:6], refs[6:]
    me = lax.axis_index("sub")
    odd = lax.rem(lax.axis_index("grp"), 2) == 1
    for shift, block in zip(SHIFTS, arrived):
        first, second, third = (off_ref[slot, me] == -shift for slot in range(NB))
        slot = jnp.where(first, 0, jnp.where(second, 1, 2))
        used = jnp.logical_or(first, jnp.logical_or(second, third))
        rows = pl.ds(pl.multiple_of((slot + 1) * NVEC, NVEC), NVEC)
        for o in range(OV):
            tile = place_ref[slot, 0, o]
            low, high = tile < RIM, tile >= TD - RIM
            spot = lanes(jnp.where(low, tile, tile - (TD - RIM)))
            rim = jnp.logical_and(used, jnp.logical_or(low, high))

            @pl.when(jnp.logical_and(rim, low == odd))
            def _():
                near[rows, spot] = tile_of(block, o)

            @pl.when(jnp.logical_and(rim, low != odd))
            def _():
                far[rows, spot] = tile_of(block, o)


def main_kernel(off_ref, place_ref, stiff, product, rest, _, *refs):
    arrived, (total, carry, basis, rows, low_rows) = refs[:4], refs[4:]
    me = lax.axis_index("sub")
    for shift, block in zip(SHIFTS, arrived):
        for slot in range(NB):

            @pl.when(off_ref[slot, me] == -shift)
            def _():
                for o in range(OV):
                    tile = place_ref[slot, 0, o]
                    basis[(slot + 1) * NVEC : (slot + 2) * NVEC, lanes(tile)] = tile_of(block, o)

    others = basis.at[NVEC:]
    rows[:NVEC] = product[:, RIM * TILE : (RIM + TD) * TILE]
    low_rows[:NVEC] = rest[...]
    for c in range(TD):
        first, second = split(row_sum(others, stiff, c))
        rows[NVEC:, c * TILE : (c + 1) * TILE] = first
        low_rows[NVEC:, c * TILE : (c + 1) * TILE] = second
    total[...] = lax.dot_general(
        rows[...], basis[...], NT, preferred_element_type=f32
    ) + lax.dot_general(low_rows[...], basis[...], NT, preferred_element_type=f32)
    carry[:NVEC, : RIM * TILE] = product[:, : RIM * TILE]
    carry[:NVEC, RIM * TILE :] = product[:, (RIM + TD) * TILE :]
    for i, c in enumerate((-2, -1, TD, TD + 1)):
        carry[NVEC:, i * TILE : (i + 1) * TILE] = row_sum(others, stiff, c).astype(bf16)


def finish_kernel(total, carry, far, near, mine, other, sums):
    layer = lax.axis_index("grp")
    odd = lax.rem(layer, 2)
    inner = jnp.logical_and(layer > 0, layer < LAYERS - 1)

    def outer(side, right):
        half = RIM * TILE
        left = carry[:, pl.ds(pl.multiple_of(side * half, half), half)]
        return lax.dot_general(left, right[...], NT, preferred_element_type=f32)

    sums[...] = total[...] + outer(1 - odd, near)

    @pl.when(inner)
    def _():
        sums[...] += outer(odd, far)

    share = COLS // LAYERS
    for x in range(LAYERS // 2):
        mine[x] = sums[pl.ds(pl.multiple_of((2 * x + odd) * share, share), share)]
        other[x] = sums[pl.ds(pl.multiple_of((2 * x + 1 - odd) * share, share), share)]


def far_moves():
    moves = []
    for sub in range(SUBS):
        for layer in range(LAYERS):
            if layer in (0, LAYERS - 1):
                to = (sub ^ 1, layer)
            else:
                to = (sub, layer + 1 if layer % 2 else layer - 1)
            moves.append((sub * LAYERS + layer, to[0] * LAYERS + to[1]))
    return moves


def swapped(value, pairs):
    return lax.ppermute(value, "grp", [p for a, b in pairs for p in ((a, b), (b, a))])


def on_device(stiffness, deflation, off_map, need_map, place_map):
    stiff, own = stiffness[0], deflation[0]
    off = off_map.T
    need = need_map.transpose(1, 2, 3, 0)[0]
    place = place_map[0].transpose(1, 0, 2)
    shape = jax.ShapeDtypeStruct

    *packed, own = kernel_call(
        pack_kernel,
        [shape((NVEC, OV * TILE), bf16)] * 4 + [pltpu.VMEM(own.shape, bf16)],
        [HBM] * 3,
        [
            pltpu.SMEM(off.shape, jnp.int32),
            pltpu.SMEM(need.shape, jnp.int32),
            pltpu.SemaphoreType.DMA((3,)),
        ],
    )(*(pltpu.with_memory_space_constraint(value, pltpu.HBM) for value in (off, need, own)))
    own = pltpu.with_memory_space_constraint(own, pltpu.VMEM)
    arrived = [
        lax.ppermute(block, "sub", [(k, (k + shift) % SUBS) for k in range(SUBS)])
        for shift, block in zip(SHIFTS, packed)
    ]
    edges = pltpu.VMEM((COLS, RIM * TILE), bf16)
    whole = pltpu.VMEM((COLS, TD * TILE), bf16)
    product, rest, *kept = kernel_call(
        own_kernel,
        [
            shape((NVEC, (TD + 2 * RIM) * TILE), bf16),
            shape((NVEC, TD * TILE), bf16),
            pltpu.VMEM(stiff.shape, bf16),
            whole,
            edges,
            edges,
        ],
        [HBM, VMEM],
        [pltpu.SemaphoreType.DMA((TD,))],
        flops=2 * NVEC * TD * BAND * TILE * TILE,
        size=2**24,
    )(pltpu.with_memory_space_constraint(stiff, pltpu.HBM), own)
    stiff, basis, near, far = (
        pltpu.with_memory_space_constraint(value, pltpu.VMEM) for value in kept
    )
    near, far = kernel_call(
        edge_kernel,
        [shape((COLS, RIM * TILE), bf16)] * 2,
        [SMEM, SMEM] + [VMEM] * 6,
        aliases={2: 0, 3: 1},
    )(off, place, near, far, *arrived)
    far = lax.ppermute(far, ("sub", "grp"), far_moves())
    near = swapped(near, [(k, k + 1) for k in range(0, LAYERS, 2)])
    total, carry, _ = kernel_call(
        main_kernel,
        [
            shape((COLS, COLS), f32),
            shape((COLS, 2 * RIM * TILE), bf16),
            shape((COLS, TD * TILE), bf16),
        ],
        [SMEM, SMEM] + [VMEM] * 8,
        [pltpu.VMEM((COLS, TD * TILE), bf16)] * 2,
        mib=24,
        flops=2 * COLS * TD * (BAND + 1) * TILE * TILE,
        size=2**22,
        aliases={5: 2},
    )(off, place, stiff, product, rest, basis, *arrived)
    part = shape((LAYERS // 2, COLS // LAYERS, COLS), f32)
    mine, other = kernel_call(
        finish_kernel, [part, part], [VMEM] * 4, [pltpu.VMEM((COLS, COLS), f32)]
    )(total, carry, far, near)
    both = mine + lax.ppermute(other, "grp", [(k, k ^ 1) for k in range(LAYERS)])
    chip = lax.shift_right_logical(lax.axis_index("grp"), 1)
    share = lax.dynamic_index_in_dim(both, chip, 0, keepdims=False)
    for step in (2, 3, 1):
        block = lax.dynamic_index_in_dim(both, chip ^ step, 0, keepdims=False)
        share = share + lax.ppermute(block, "grp", [(k, k ^ (2 * step)) for k in range(LAYERS)])
    return share[None]


def solution(mesh):
    in_specs = (
        P("sub", "grp", None, None, None),
        P("sub", None, "grp"),
        P(),
        P(None, "grp", None, None),
        P("sub", "grp", None, None),
    )
    out_specs = P("sub", "grp", None)
    return jax.shard_map(
        on_device, mesh=mesh, in_specs=in_specs, out_specs=out_specs, check_vma=False
    )
```
